32 devices in a mesh: wide: 8 (over z, x), tensor: 4 (over y, core).
Axes of the slice: x: 2, y: 2, z: 4, core: 2. Of those that a mesh axis runs over, the one named last changes fastest.
Arguments:
- tokens: bfloat16 [16, 1024, 768], P('wide', 'tensor'), may hold values from -6 to 6
- cotangent: bfloat16 [16, 1024, 768], P('wide', 'tensor'), may hold values from -6 to 6
- ln1_gain: bfloat16 [2, 768], P(None, 'wide'), may hold values from 0.25 to 1.75
- ln1_bias: bfloat16 [2, 768], P(None, 'wide'), may hold values from -3 to 3
- ln2_gain: bfloat16 [2, 768], P(None, 'wide'), may hold values from 0.25 to 1.75
- ln2_bias: bfloat16 [2, 768], P(None, 'wide'), may hold values from -3 to 3
- qkv_weight: bfloat16 [2, 3, 768, 768], P(None, None, 'wide', 'tensor'), may hold values from -0.21875 to 0.21875
- qkv_bias: bfloat16 [2, 3, 12, 64], P(None, None, 'tensor', 'wide'), may hold values from -3 to 3
- dense_weight: bfloat16 [2, 768, 768], P(None, 'tensor', 'wide'), may hold values from -1.75 to 1.75
- dense_bias: bfloat16 [2, 768], P(None, 'wide'), may hold values from -3 to 3
- fc1_weight: bfloat16 [2, 768, 3072], P(None, 'wide', 'tensor'), may hold values from -0.21875 to 0.21875
- fc1_bias: bfloat16 [2, 12, 256], P(None, 'tensor', 'wide'), may hold values from -3 to 3
- fc2_weight: bfloat16 [2, 3072, 768], P(None, 'tensor', 'wide'), may hold values from -0.109375 to 0.109375
- fc2_bias: bfloat16 [2, 768], P(None, 'wide'), may hold values from -3 to 3
Outputs:
- mixed: bfloat16 [16, 1024, 768], P('wide', 'tensor')
- input_grad: bfloat16 [16, 1024, 768], P('wide', 'tensor')
- ln1_gain_grad: float32 [2, 768], P(None, 'wide')
- ln1_bias_grad: float32 [2, 768], P(None, 'wide')
- ln2_gain_grad: float32 [2, 768], P(None, 'wide')
- ln2_bias_grad: float32 [2, 768], P(None, 'wide')
- qkv_weight_grad: float32 [2, 3, 768, 768], P(None, None, 'wide', 'tensor')
- qkv_bias_grad: float32 [2, 3, 12, 64], P(None, None, 'tensor', 'wide')
- dense_weight_grad: float32 [2, 768, 768], P(None, 'tensor', 'wide')
- dense_bias_grad: float32 [2, 768], P(None, 'wide')
- fc1_weight_grad: float32 [2, 768, 3072], P(None, 'wide', 'tensor')
- fc1_bias_grad: float32 [2, 12, 256], P(None, 'tensor', 'wide')
- fc2_weight_grad: float32 [2, 3072, 768], P(None, 'tensor', 'wide')
- fc2_bias_grad: float32 [2, 768], P(None, 'wide')
The draws below stay inside these ranges and needn't reach their ends.
All inputs are finite; a program needn't handle non-finite values.
Results may differ from the reference program's by a relative error of at most 0.018.
Values may be sent and summed in bfloat16 or wider, within the bound.
A program may use at most 256 MiB of HBM per device.

```python
import math
import jax
import jax.numpy as jnp
from jax import lax

D = 768
HEADS = 12
HD = 64
FF = 3072
ROT = 16
LAYERS = 2
LEN = 1024
SEQS = 16


def spiked(values, key, source, target, shards_of, factor):
    def block_of(axis_at):
        return (jnp.arange(values.shape[axis_at]) // (values.shape[axis_at] // shards_of)).reshape((-1,) + (1,) * (values.ndim - 1 - axis_at))

    near = jax.random.permutation(key, shards_of)[block_of(target)]
    other_side = (block_of(target) + shards_of // 2) % shards_of
    return jnp.where((block_of(source) == near) | (block_of(source) == other_side), factor * values, values)


def shard_levels(stream_key, dims, pieces, low, top_value):
    gain = 1.0
    for dim, shards_of in pieces:
        steps = jax.random.uniform(jax.random.fold_in(jax.random.fold_in(stream_key, 6), dim), (shards_of,), jnp.float32, low / len(pieces), top_value / len(pieces))
        gain = gain * jnp.repeat(jnp.exp(steps), dims[dim] // shards_of).reshape((-1,) + (1,) * (len(dims) - 1 - dim))
    return gain


def normal_values(own_key, shape, spread, reach, pieces=(), kind=jnp.bfloat16):
    drawn = spread * jax.random.normal(own_key, shape, jnp.float32)
    if pieces:
        drawn = drawn * shard_levels(own_key, shape, pieces, -0.22, 0.18)
    return jnp.clip(drawn, -reach, reach).astype(kind)


def noise_with(rng, shape, spread, limit, cuts, heavy, kind=jnp.bfloat16):
    drawn = spread * jax.random.normal(rng, shape, jnp.float32)
    if cuts:
        drawn = drawn * shard_levels(rng, shape, cuts, -0.22, 0.18)
    return jnp.clip(spiked(drawn, jax.random.fold_in(rng, 3), *heavy), -limit, limit).astype(kind)


def setup_inputs(seed: int = 0) -> dict:
    streams_of = jax.random.split(jax.random.key(seed), 15)
    tokens = noise_with(streams_of[0], (SEQS, LEN, D), 1.0, 6.0, ((0, 8), (1, 4)), (0, 2, 8, 2.0))
    cotangent = noise_with(streams_of[1], (SEQS, LEN, D), 1.0, 6.0, ((0, 8), (1, 4)), (0, 2, 8, 2.0))
    ln1_gain = jnp.clip(1.0 + 0.15 * jax.random.normal(streams_of[2], (LAYERS, D), jnp.float32), 0.25, 1.75).astype(jnp.bfloat16)
    ln1_bias = normal_values(streams_of[3], (LAYERS, D), 0.5, 3.0, ((1, 8),))
    ln2_gain = jnp.clip(1.0 + 0.15 * jax.random.normal(streams_of[4], (LAYERS, D), jnp.float32), 0.25, 1.75).astype(jnp.bfloat16)
    ln2_bias = normal_values(streams_of[5], (LAYERS, D), 0.5, 3.0, ((1, 8),))
    qkv_weight = normal_values(streams_of[6], (LAYERS, 3, D, HEADS * HD), D ** -0.5, 0.21875, ((2, 8), (3, 4)))
    qkv_bias = normal_values(streams_of[7], (LAYERS, 3, HEADS, HD), 0.5, 3.0, ((2, 4), (3, 8)))
    dense_weight = normal_values(streams_of[8], (LAYERS, HEADS * HD, D), (D // 64) ** -0.5, 1.75, ((1, 4), (2, 8)))
    dense_bias = normal_values(streams_of[9], (LAYERS, D), 0.5, 3.0, ((1, 8),))
    fc1_weight = normal_values(streams_of[10], (LAYERS, D, FF), D ** -0.5, 0.21875, ((1, 8), (2, 4)))
    fc1_bias = normal_values(streams_of[11], (LAYERS, HEADS, FF // HEADS), 0.5, 3.0, ((1, 4), (2, 8)))
    fc2_weight = normal_values(streams_of[12], (LAYERS, FF, D), FF ** -0.5, 0.109375, ((1, 4), (2, 8)))
    fc2_bias = normal_values(streams_of[13], (LAYERS, D), 0.5, 3.0, ((1, 8),))
    return dict(tokens=tokens, cotangent=cotangent, ln1_gain=ln1_gain, ln1_bias=ln1_bias, ln2_gain=ln2_gain, ln2_bias=ln2_bias, qkv_weight=qkv_weight, qkv_bias=qkv_bias, dense_weight=dense_weight, dense_bias=dense_bias, fc1_weight=fc1_weight, fc1_bias=fc1_bias, fc2_weight=fc2_weight, fc2_bias=fc2_bias)


@jax.custom_vjp
def low(v):
    return lax.optimization_barrier(v.astype(jnp.bfloat16)).astype(jnp.float32)

@jax.custom_vjp
def lower_backward(v):
    return v

def low_keep(v):
    return (low(v), None)

def low_pass(kept, grad):
    return (grad,)

def back_keep(v):
    return (v, None)

def back_low(kept, grad):
    return (low(grad),)
low.defvjp(low_keep, low_pass)
lower_backward.defvjp(back_keep, back_low)
EPSILON = 1e-05
HIGHEST_EXACTNESS = lax.Precision.HIGHEST

def rotary_tables(seq_len):
    half_rot = ROT // 2
    positions = jnp.arange(seq_len, dtype=jnp.float32)
    freq_index = jnp.arange(half_rot, dtype=jnp.float32)
    inverse = jnp.exp(freq_index * (-2.0 * math.log(10000.0) / ROT))
    angles = positions[:, None] * inverse[None, :]
    return (jnp.cos(angles)[:, None, :], jnp.sin(angles)[:, None, :])

def rotate(values, cos_tab, sin_tab):
    half_rot = ROT // 2
    front_half = values[..., :half_rot]
    second = values[..., half_rot:ROT]
    return jnp.concatenate([front_half * cos_tab - second * sin_tab, second * cos_tab + front_half * sin_tab, values[..., ROT:]], axis=-1)

def normalize(residual, gain_vec, shift_vec):
    mean_val = lax.optimization_barrier(jnp.mean(residual, axis=-1, keepdims=True))
    centered = residual - mean_val
    variance = lax.optimization_barrier(jnp.mean(centered * centered, axis=-1, keepdims=True))
    return centered * lax.rsqrt(variance + EPSILON) * gain_vec + shift_vec

def layer_forward(residual, params, cos_tab, sin_tab, causal):
    gain_a, shift_a, gain_b, shift_b, query_key_value_weight, query_key_value_bias, output_weight, out_b, up_weight, up_bias, down_weight, down_b = params
    seqs_n, seq_len, width = residual.shape
    first_norm_rows = low(normalize(residual, gain_a, shift_a))
    second_norm_rows = low(normalize(residual, gain_b, shift_b))
    linear_rows = jnp.einsum('ahf,gft->gaht', first_norm_rows, query_key_value_weight, precision=HIGHEST_EXACTNESS) + query_key_value_bias[:, None, None, :]
    linear_rows = lower_backward(linear_rows)
    linear_rows = linear_rows.reshape(3, seqs_n, seq_len, HEADS, HD)
    queries = low(rotate(linear_rows[0], cos_tab, sin_tab))
    key_rows = low(rotate(linear_rows[1], cos_tab, sin_tab))
    value_rows = low(linear_rows[2])
    scores = jnp.einsum('sqhe,skhe->shqk', queries, key_rows, precision=HIGHEST_EXACTNESS) * (1.0 / math.sqrt(HD))
    scores = lower_backward(jnp.where(causal, scores, -1e+30))
    prob_rows = jax.nn.softmax(scores, axis=-1)
    head_output_rows = jnp.einsum('shqk,skhe->sqhe', low(prob_rows), value_rows, precision=HIGHEST_EXACTNESS)
    head_output_rows = low(lower_backward(head_output_rows.reshape(seqs_n, seq_len, HEADS * HD)))
    attention_result = jnp.einsum('bwk,kx->bwx', head_output_rows, output_weight, precision=HIGHEST_EXACTNESS)
    hidden_rows = lower_backward(jnp.einsum('kwc,ci->kwi', second_norm_rows, up_weight, precision=HIGHEST_EXACTNESS) + up_bias)
    activated_hidden = low(jax.nn.gelu(hidden_rows, approximate=False))
    branch_output = lower_backward(attention_result + jnp.einsum('prc,ck->prk', activated_hidden, down_weight, precision=HIGHEST_EXACTNESS))
    return residual + branch_output + out_b + down_b

def reference(tokens, cotangent, ln1_gain, ln1_bias, ln2_gain, ln2_bias, qkv_weight, qkv_bias, dense_weight, dense_bias, fc1_weight, fc1_bias, fc2_weight, fc2_bias):
    weights = (ln1_gain.astype(jnp.float32), ln1_bias.astype(jnp.float32), ln2_gain.astype(jnp.float32), ln2_bias.astype(jnp.float32), qkv_weight.astype(jnp.float32), qkv_bias.astype(jnp.float32).reshape(LAYERS, 3, HEADS * HD), dense_weight.astype(jnp.float32), dense_bias.astype(jnp.float32), fc1_weight.astype(jnp.float32), fc1_bias.astype(jnp.float32).reshape(LAYERS, FF), fc2_weight.astype(jnp.float32), fc2_bias.astype(jnp.float32))
    cos_tab, sin_tab = rotary_tables(LEN)
    causal = jnp.arange(LEN)[:, None] >= jnp.arange(LEN)[None, :]

    def model(residual, params):
        for layer_idx in range(LAYERS):
            residual = layer_forward(residual, tuple((weight_arr[layer_idx] for weight_arr in params)), cos_tab, sin_tab, causal)
        return residual
    group_size = math.gcd(SEQS, max(1, 4096 // LEN))
    group_count = SEQS // group_size
    inputs = tokens.astype(jnp.float32).reshape(group_count, group_size, LEN, D)
    cots = cotangent.astype(jnp.float32).reshape(group_count, group_size, LEN, D)
    zero_sums = tuple((jnp.zeros_like(weight_arr) for weight_arr in weights))

    def step(totals, batch_pair):
        seq_in, seq_cot = batch_pair
        result, pullback = jax.vjp(model, seq_in, weights)
        grad_in, grad_weights = pullback(seq_cot)
        totals = tuple((left_sum + right_sum for left_sum, right_sum in zip(totals, grad_weights)))
        return (totals, (result.astype(jnp.bfloat16), grad_in.astype(jnp.bfloat16)))
    totals, (outs_all, grads_all) = lax.scan(step, zero_sums, (inputs, cots))
    mixed = outs_all.reshape(SEQS, LEN, D)
    input_grad = grads_all.reshape(SEQS, LEN, D)
    return (mixed, input_grad, totals[0], totals[1], totals[2], totals[3], totals[4], totals[5].reshape(LAYERS, 3, HEADS, HD), totals[6], totals[7], totals[8], totals[9].reshape(LAYERS, HEADS, FF // HEADS), totals[10], totals[11])
```

```python
import math

import jax
import jax.numpy as jnp
from jax import lax
from jax.experimental import pallas as pl
from jax.experimental.pallas import tpu as pltpu
from jax.sharding import PartitionSpec as P

HD = 64
ROT = 16
EPSILON = 1e-05
Q_ROWS = 256
BF = jnp.bfloat16
F32 = jnp.float32

NN = (((1,), (0,)), ((), ()))
NT = (((1,), (1,)), ((), ()))
TN = (((0,), (0,)), ((), ()))


def dot(a, b, dims):
    return lax.dot_general(a, b, dims, preferred_element_type=F32)


def rotary_planes(seq_len, heads):
    half = ROT // 2
    positions = jnp.arange(seq_len, dtype=F32)
    inverse = jnp.exp(jnp.arange(half, dtype=F32) * (-2.0 * math.log(10000.0) / ROT))
    angles = positions[:, None] * inverse[None, :]
    cos, sin = jnp.cos(angles), jnp.sin(angles)
    zero = jnp.zeros((seq_len, half), F32)
    rest0 = jnp.zeros((seq_len, HD - ROT), F32)
    same = jnp.concatenate([cos, cos, rest0 + 1.0], axis=1)
    ahead = jnp.concatenate([-sin, zero, rest0], axis=1)
    behind = jnp.concatenate([zero, sin, rest0], axis=1)

    def spread(plane, fill):
        return jnp.concatenate(
            [jnp.tile(plane, (1, 2 * heads)), jnp.full((seq_len, heads * HD), fill, F32)], axis=1
        )

    return spread(same, 1.0), spread(ahead, 0.0), spread(behind, 0.0)


def rotate(u, planes, sign):
    same, ahead, behind = planes
    half = ROT // 2
    return u * same + sign * (
        jnp.roll(u, -half, axis=1) * ahead + jnp.roll(u, half, axis=1) * behind
    )


def transposed_probs(q, k, row0, end):
    rows = q.shape[0]
    scores = dot(k, q, NT) * (1.0 / math.sqrt(HD))
    key_pos = lax.broadcasted_iota(jnp.int32, (end, rows), 0)
    query_pos = row0 + lax.broadcasted_iota(jnp.int32, (end, rows), 1)
    scores = jnp.where(key_pos <= query_pos, scores, -1e30)
    exps = jnp.exp(scores - jnp.max(scores, axis=0, keepdims=True))
    return exps * (1.0 / jnp.sum(exps, axis=0, keepdims=True))


def attend_kernel(heads, qkv_ref, out_ref):
    seq_len = qkv_ref.shape[0]
    width = heads * HD
    for h in range(heads):
        lanes = slice(h * HD, (h + 1) * HD)
        for row0 in range(0, seq_len, Q_ROWS):
            end = row0 + Q_ROWS
            q = qkv_ref[row0:end, h * HD:(h + 1) * HD]
            k = qkv_ref[0:end, width + h * HD:width + (h + 1) * HD]
            v = qkv_ref[0:end, 2 * width + h * HD:2 * width + (h + 1) * HD]
            probs = transposed_probs(q, k, row0, end).astype(BF)
            out_ref[row0:end, lanes] = dot(v, probs, TN).T.astype(BF)


def attend_back_kernel(heads, qkv_ref, grad_ref, out_ref):
    seq_len = qkv_ref.shape[0]
    width = heads * HD
    scale = 1.0 / math.sqrt(HD)
    for h in range(heads):
        lq = slice(h * HD, (h + 1) * HD)
        lk = slice(width + h * HD, width + (h + 1) * HD)
        lv = slice(2 * width + h * HD, 2 * width + (h + 1) * HD)
        for row0 in reversed(range(0, seq_len, Q_ROWS)):
            end = row0 + Q_ROWS
            q = qkv_ref[row0:end, lq]
            k = qkv_ref[0:end, lk]
            v = qkv_ref[0:end, lv]
            d_out = grad_ref[row0:end, lq]
            probs = transposed_probs(q, k, row0, end)
            d_probs = dot(v, d_out, NT)
            delta = jnp.sum(probs * d_probs, axis=0, keepdims=True)
            d_scores = (probs * (d_probs - delta)).astype(BF)
            out_ref[row0:end, lq] = dot(k, d_scores, TN).T * scale
            d_k = dot(d_scores, q, NN) * scale
            d_v = dot(probs.astype(BF), d_out, NN)
            if end == seq_len:
                out_ref[:, lk] = d_k
                out_ref[:, lv] = d_v
            else:
                out_ref[0:end, lk] = out_ref[0:end, lk] + d_k
                out_ref[0:end, lv] = out_ref[0:end, lv] + d_v


def whole_blocks(count):
    return [pl.BlockSpec(memory_space=pltpu.VMEM)] * count


def attend(qkv, heads):
    seq_len = qkv.shape[0]

    def run(qkv_ref, out_ref):
        attend_kernel(heads, qkv_ref, out_ref)

    return pl.pallas_call(
        run,
        out_shape=jax.ShapeDtypeStruct((seq_len, heads * HD), BF),
        in_specs=whole_blocks(1),
        out_specs=whole_blocks(1)[0],
        compiler_params=pltpu.CompilerParams(vmem_limit_bytes=32 * 2**20),
        cost_estimate=pl.CostEstimate(
            flops=4 * heads * seq_len * seq_len * HD,
            bytes_accessed=8 * seq_len * heads * HD,
            transcendentals=heads * seq_len * seq_len // 2,
        ),
    )(qkv)


def attend_back(qkv, grad_heads, heads):
    seq_len = qkv.shape[0]

    def run(qkv_ref, grad_ref, out_ref):
        attend_back_kernel(heads, qkv_ref, grad_ref, out_ref)

    return pl.pallas_call(
        run,
        out_shape=jax.ShapeDtypeStruct((seq_len, 3 * heads * HD), F32),
        in_specs=whole_blocks(2),
        out_specs=whole_blocks(1)[0],
        compiler_params=pltpu.CompilerParams(vmem_limit_bytes=32 * 2**20),
        cost_estimate=pl.CostEstimate(
            flops=10 * heads * seq_len * seq_len * HD,
            bytes_accessed=20 * seq_len * heads * HD,
            transcendentals=heads * seq_len * seq_len // 2,
        ),
    )(qkv, grad_heads)


def normalize_rows(residual):
    mean_val = jnp.mean(residual, axis=-1, keepdims=True)
    centered = residual - mean_val
    variance = jnp.mean(centered * centered, axis=-1, keepdims=True)
    inv_std = lax.rsqrt(variance + EPSILON)
    return centered * inv_std, inv_std


def swap(x, bit, size):
    return lax.ppermute(x, "tensor", [(i, i ^ bit) for i in range(size)])


def gather_rows(x, size):
    me = lax.axis_index("tensor")
    far = swap(x, 2, size)
    parts = [x, swap(x, 1, size), far, swap(far, 1, size)]
    rows = x.shape[0]
    full = jnp.zeros((size * rows,) + x.shape[1:], x.dtype)
    for k, part in enumerate(parts):
        full = lax.dynamic_update_slice(full, part, ((me ^ k) * rows, 0))
    return full


def scatter_rows(partial, size):
    me = lax.axis_index("tensor")
    core, chip = me % 2, me // 2
    rows = partial.shape[0] // size
    pieces = partial.reshape(2, 2, rows, partial.shape[1])
    away = lax.dynamic_index_in_dim(pieces, 1 - core, 1, keepdims=False)
    kept = lax.dynamic_index_in_dim(pieces, core, 1, keepdims=False)
    both = kept.astype(F32) + swap(away, 1, size).astype(F32)
    off = lax.dynamic_index_in_dim(both, 1 - chip, 0, keepdims=False).astype(BF)
    mine = lax.dynamic_index_in_dim(both, chip, 0, keepdims=False)
    return mine + swap(off, 2, size).astype(F32)


def gather_weights(x):
    return lax.all_gather(x, "wide", axis=0, tiled=True)


def sum_to_owner(x, size):
    rows = x.shape[0] // size
    pieces = x.astype(BF).reshape(size, rows, x.shape[1])
    return jnp.sum(
        lax.all_to_all(pieces, "wide", 0, 0).astype(F32), axis=0
    )


def body(
    tokens,
    cotangent,
    ln1_gain,
    ln1_bias,
    ln2_gain,
    ln2_bias,
    qkv_weight,
    qkv_bias,
    dense_weight,
    dense_bias,
    fc1_weight,
    fc1_bias,
    fc2_weight,
    fc2_bias,
):
    wide = lax.axis_size("wide")
    tensor = lax.axis_size("tensor")
    w_me = lax.axis_index("wide")
    layers = qkv_weight.shape[0]
    seqs = tokens.shape[0]
    local_len, model = tokens.shape[1:]
    seq_len = local_len * tensor
    own = ln1_gain.shape[1]
    heads = qkv_bias.shape[2]
    groups = fc1_bias.shape[1]
    att = heads * HD
    hid = fc1_weight.shape[2]
    planes = rotary_planes(seq_len, heads)

    first_own, w1, w2, offset_parts = [], [], [], []
    for l in range(layers):
        qkv_own = jnp.concatenate([qkv_weight[l, c] for c in range(3)], axis=1)
        up_own = fc1_weight[l]
        first_own.append((up_own.astype(F32), qkv_own.astype(F32)))
        folded = jnp.concatenate(
            [
                up_own.astype(F32) * ln2_gain[l].astype(F32)[:, None],
                qkv_own.astype(F32) * ln1_gain[l].astype(F32)[:, None],
            ],
            axis=1,
        ).astype(BF)
        w1.append(gather_weights(folded))
        w2.append(
            gather_weights(jnp.concatenate([fc2_weight[l].T, dense_weight[l].T], axis=1))
        )
        up_b = jnp.zeros((groups, hid // groups), F32)
        up_b = lax.dynamic_update_slice(
            up_b, fc1_bias[l].astype(F32), (0, w_me * fc1_bias.shape[2])
        )
        qkv_b = jnp.zeros((3, heads, HD), F32)
        qkv_b = lax.dynamic_update_slice(
            qkv_b, qkv_bias[l].astype(F32), (0, 0, w_me * qkv_bias.shape[3])
        )
        out_b = jnp.zeros((model,), F32)
        out_b = lax.dynamic_update_slice(
            out_b, dense_bias[l].astype(F32) + fc2_bias[l].astype(F32), (w_me * own,)
        )
        shift_b = jnp.sum(ln2_bias[l].astype(F32)[:, None] * up_own.astype(F32), axis=0)
        shift_a = jnp.sum(ln1_bias[l].astype(F32)[:, None] * qkv_own.astype(F32), axis=0)
        offset_parts.append(
            jnp.concatenate([shift_b + up_b.reshape(-1), shift_a + qkv_b.reshape(-1), out_b])
        )
    offsets = lax.psum(jnp.stack(offset_parts), "wide")

    residual = [tokens[s].astype(F32) for s in range(seqs)]
    saved = []
    for l in range(layers):
        up_off = offsets[l, :hid]
        qkv_off = offsets[l, hid:hid + 3 * att]
        out_off = offsets[l, hid + 3 * att:]
        per_seq = []
        for s in range(seqs):
            scaled, inv_std = normalize_rows(residual[s])
            if l == 0:
                full_tokens = gather_rows(tokens[s], tensor)
                full = normalize_rows(full_tokens.astype(F32))[0].astype(BF)
            else:
                full = gather_rows(scaled.astype(BF), tensor)
            lin = dot(full, w1[l][:, hid:], NN) + qkv_off
            qkv = rotate(lin, planes, 1.0).astype(BF)
            heads_out = attend(qkv, heads)
            hidden = dot(full, w1[l][:, :hid], NN) + up_off
            phi = 0.5 + 0.5 * lax.erf(hidden * math.sqrt(0.5))
            act = (hidden * phi).astype(BF)
            slope = (
                phi + hidden * jnp.exp(-0.5 * hidden * hidden) * (1.0 / math.sqrt(2.0 * math.pi))
            ).astype(BF)
            partial = dot(act, w2[l][:, :hid], NT) + dot(heads_out, w2[l][:, hid:], NT)
            branch = scatter_rows(partial.astype(BF), tensor)
            residual[s] = residual[s] + branch + out_off
            per_seq.append((scaled, inv_std, full, qkv, heads_out, act, slope))
        saved.append(per_seq)
    mixed = jnp.stack([r.astype(BF) for r in residual])

    grad = [cotangent[s].astype(F32) for s in range(seqs)]
    outs = [None] * layers
    for l in reversed(range(layers)):
        bias_part = sum(jnp.sum(g, axis=0) for g in grad)
        w_up, w_qkv = w1[l][:, :hid], w1[l][:, hid:]
        w_down, w_out = w2[l][:, :hid], w2[l][:, hid:]
        full_grad, d_hid, d_lin = [], [], []
        for s in range(seqs):
            scaled, inv_std, full, qkv, heads_out, act, slope = saved[l][s]
            g_full = gather_rows(grad[s].astype(BF), tensor)
            d_heads = dot(g_full, w_out, NN).astype(BF)
            d_hidden = (dot(g_full, w_down, NN) * slope.astype(F32)).astype(BF)
            d_qkv = rotate(attend_back(qkv, d_heads, heads), planes, -1.0).astype(BF)
            e_part = dot(d_hidden, w_up, NT) + dot(d_qkv, w_qkv, NT)
            e = scatter_rows(e_part.astype(BF), tensor)
            mean_e = jnp.mean(e, axis=-1, keepdims=True)
            mean_x = jnp.mean(e * scaled, axis=-1, keepdims=True)
            grad[s] = grad[s] + inv_std * (e - mean_e - scaled * mean_x)
            full_grad.append(g_full)
            d_hid.append(d_hidden)
            d_lin.append(d_qkv)
        grads_of = lambda lefts, rights: sum(dot(a, b, TN) for a, b in zip(lefts, rights))
        fulls = [saved[l][s][2] for s in range(seqs)]
        down_grad = sum_to_owner(grads_of(full_grad, [saved[l][s][5] for s in range(seqs)]), wide)
        out_grad = sum_to_owner(grads_of(full_grad, [saved[l][s][4] for s in range(seqs)]), wide)
        up_raw = sum_to_owner(grads_of(fulls, d_hid), wide)
        qkv_raw = sum_to_owner(grads_of(fulls, d_lin), wide)
        up_db = sum(jnp.sum(d.astype(F32), axis=0) for d in d_hid)
        qkv_db = sum(jnp.sum(d.astype(F32), axis=0) for d in d_lin)
        outs[l] = (down_grad, out_grad, up_raw, qkv_raw, up_db, qkv_db, bias_part)
    input_grad = jnp.stack([g.astype(BF) for g in grad])

    db_all = lax.psum(
        jnp.stack([jnp.concatenate([outs[l][4], outs[l][5]]) for l in range(layers)]), "wide"
    )
    bias_all = lax.psum(jnp.stack([outs[l][6] for l in range(layers)]), ("wide", "tensor"))
    out_bias_grad = lax.dynamic_slice(bias_all, (0, w_me * own), (layers, own))
    norm_parts, weight_grads = [], []
    for l in range(layers):
        down_grad, out_grad, up_raw, qkv_raw = outs[l][:4]
        up_db, qkv_db = db_all[l, :hid], db_all[l, hid:]
        up_own, qkv_own = first_own[l]
        norm_parts.append(
            jnp.stack(
                [
                    jnp.sum(qkv_raw * qkv_own, axis=1),
                    jnp.sum(qkv_own * qkv_db[None, :], axis=1),
                    jnp.sum(up_raw * up_own, axis=1),
                    jnp.sum(up_own * up_db[None, :], axis=1),
                ]
            )
        )
        col = lambda v: v[l].astype(F32)[:, None]
        up_grad = col(ln2_gain) * up_raw + col(ln2_bias) * up_db[None, :]
        qkv_grad = col(ln1_gain) * qkv_raw + col(ln1_bias) * qkv_db[None, :]
        qkv_grad = jnp.stack([qkv_grad[:, c * att:(c + 1) * att] for c in range(3)])
        qkv_bg = lax.dynamic_slice(
            qkv_db.reshape(3, heads, HD), (0, 0, w_me * qkv_bias.shape[3]),
            (3, heads, qkv_bias.shape[3]),
        )
        up_bg = lax.dynamic_slice(
            up_db.reshape(groups, -1), (0, w_me * fc1_bias.shape[2]), (groups, fc1_bias.shape[2])
        )
        weight_grads.append((qkv_grad, qkv_bg, out_grad.T, up_grad, up_bg, down_grad.T))
    norms = lax.psum(jnp.stack(norm_parts), "tensor")
    wg = [jnp.stack([weight_grads[l][m] for l in range(layers)]) for m in range(6)]
    return (
        mixed,
        input_grad,
        norms[:, 0],
        norms[:, 1],
        norms[:, 2],
        norms[:, 3],
        wg[0],
        wg[1],
        wg[2],
        out_bias_grad,
        wg[3],
        wg[4],
        wg[5],
        out_bias_grad,
    )


def solution(mesh):
    specs = (
        P("wide", "tensor", None),
        P("wide", "tensor", None),
        P(None, "wide"),
        P(None, "wide"),
        P(None, "wide"),
        P(None, "wide"),
        P(None, None, "wide", "tensor"),
        P(None, None, "tensor", "wide"),
        P(None, "tensor", "wide"),
        P(None, "wide"),
        P(None, "wide", "tensor"),
        P(None, "tensor", "wide"),
        P(None, "tensor", "wide"),
        P(None, "wide"),
    )
    return jax.shard_map(body, mesh=mesh, in_specs=specs, out_specs=specs, check_vma=False)
```
